32 devices in a mesh: groups: 2 (over y), seq: 4 (over x, core), mp: 4 (over z).
Axes of the slice: x: 2, y: 2, z: 4, core: 2. Of those that a mesh axis runs over, the one named last changes fastest.
Arguments:
- queries: bfloat16 [512, 3584], P(('groups', 'seq')), parts along dimension 0, may hold values from -5 to 5
- keys: bfloat16 [512, 512], P(('groups', 'seq')), parts along dimension 0, may hold values from -5 to 5
- values: bfloat16 [512, 512], P(('groups', 'seq')), parts along dimension 0, may hold values from -6 to 6
- hidden_in: bfloat16 [512, 3584], P(('groups', 'seq')), parts along dimension 0, may hold values from -6 to 6
- doc_ids: int32 [512], P(('groups', 'seq')), parts along dimension 0, may hold values from 0 to 7, never falling along the last dimension, each value on 1 to 128 neighbouring positions
- modality: int32 [512], P(('groups', 'seq')), parts along dimension 0, may hold values from 0 to 1, as said below
- input_weights: bfloat16 [3584, 2, 37888], P(None, None, ('seq', 'mp')), may hold values from -0.09375 to 0.09375
- output_weights: bfloat16 [37888, 3584], P(('seq', 'mp')), may hold values from -0.046875 to 0.046875
- norm_gains: float32 [2, 3584], replicated, may hold values from 0.5 to 1.5
Outputs:
- layer_out: bfloat16 [512, 3584], P(('groups', 'seq')), parts along dimension 0
The draws below stay inside these ranges and needn't reach their ends.
There are 2 independent parts, one for each index of `groups`. The reference program is written for one: setup_inputs(seed, part) draws one part's arguments, and reference() takes and returns one part's arrays. A program takes and returns all parts, laid end to end along the dimension named above; an argument that names none is the same for every part. Nothing has to cross between parts.
Inputs may be any that keep to these rules, and one draw needn't show every extreme that they name: Exactly 224 tokens have modality 1; the modality is constant on each aligned block of 16 tokens. `doc_ids`: never falls along the batch; every document has 1 to 128 tokens.
All inputs are finite; a program needn't handle non-finite values.
Results may differ from the reference program's by a relative error of at most 0.0059.
Values may be sent and summed in bfloat16 or wider, within the bound.
A program may use at most 256 MiB of HBM per device.

```python
import math
import jax
import jax.numpy as jnp
import numpy as np
from jax import lax

D = 3584
QUERY_HEADS = 28
KEY_VALUE_HEADS = 4
HEAD_SIZE = 128
FF = 18944
DOCS = 8
PACKED_TOKENS = 256
IMG_ROWS = 224


def draw_queries(key, part):
    base_offset = jnp.clip(jax.random.normal(jax.random.fold_in(key, 1), (PACKED_TOKENS, QUERY_HEADS * HEAD_SIZE), jnp.float32), -4.5, 4.5)
    return base_offset.astype(jnp.bfloat16)


def draw_keys(key, part):
    base_offset = jnp.clip(jax.random.normal(jax.random.fold_in(key, 2), (PACKED_TOKENS, KEY_VALUE_HEADS * HEAD_SIZE), jnp.float32), -4.5, 4.5)
    return base_offset.astype(jnp.bfloat16)


def draw_modality(key, part):
    shuffled = jax.random.permutation(jax.random.fold_in(key, 5), 16)
    block_kind = (shuffled >= 2).astype(jnp.int32)
    return jnp.repeat(block_kind, PACKED_TOKENS // 16)


def shard_levels(stream_key, dims, shards, low, largest):
    loudness, own = 1.0, jax.random.fold_in(stream_key, 6)
    for dim, parts in shards:
        steps = jnp.exp(jax.random.uniform(jax.random.fold_in(own, dim), (parts,), jnp.float32, low / len(shards), largest / len(shards)))
        loudness = loudness * jnp.repeat(steps, dims[dim] // parts).reshape([-1 if axis == dim else 1 for axis in range(len(dims))])
    return loudness


def split_up(amount, total, bound, lean):
    loads = [(1 << 20) // math.isqrt(standing ** lean) + 1 for standing in range(2, amount + 1)]
    spare, given = total - bound - (amount - 1), [1] * (amount - 1)
    while spare > 0:
        candidates = [i for i in range(amount - 1) if given[i] < bound]
        whole, left = sum([loads[i] for i in candidates]), spare
        for i in candidates:
            more = min(bound - given[i], max(1, left * loads[i] // whole), spare)
            given[i] = given[i] + more
            spare = spare - more
    return np.array([bound] + given)


def ragged_sizes(rng, number_of, total, bound, slope):
    if number_of == 2:
        one = jax.random.randint(rng, (), max(1, total - bound), min(bound, total - 1) + 1)
        return jnp.stack([one, total - one])
    lengths = jnp.asarray(split_up(number_of, total, bound, slope), jnp.int32)
    pairs = (number_of - 1) // 2
    giver, receiver = lengths[1:1 + 2 * pairs:2], lengths[2:2 + 2 * pairs:2]
    margin = jnp.minimum(giver - 1, bound - receiver)
    shifted = jax.random.randint(jax.random.fold_in(rng, 1), (pairs,), 0, 1 << 20) % (margin + 1)
    lengths = lengths.at[1:1 + 2 * pairs:2].set(giver - shifted).at[2:2 + 2 * pairs:2].set(receiver + shifted)
    return lengths[jax.random.permutation(jax.random.fold_in(rng, 2), number_of)]


def scatter_about(stream_key, shape, scale, reach, cuts=(), kind=jnp.bfloat16):
    values = scale * jax.random.normal(stream_key, shape, jnp.float32)
    if cuts:
        values = values * shard_levels(stream_key, shape, cuts, -0.22, 0.18)
    return jnp.clip(values, -reach, reach).astype(kind)


def setup_inputs(seed: int = 0, part: int = 0) -> dict:
    arg_keys = jax.random.split(jax.random.key(seed), 10)
    part_splits = jax.random.split(jax.random.fold_in(arg_keys[9], part), 10)
    return {
        "queries": draw_queries(jax.random.fold_in(jax.random.fold_in(arg_keys[9], part), 71), part),
        "keys": draw_keys(jax.random.fold_in(jax.random.fold_in(arg_keys[9], part), 71), part),
        "values": scatter_about(part_splits[2], (PACKED_TOKENS, KEY_VALUE_HEADS * HEAD_SIZE), 1.0, 6.0, ((0, 4),)),
        "hidden_in": scatter_about(part_splits[3], (PACKED_TOKENS, D), 1.0, 6.0, ((0, 4),)),
        "doc_ids": jnp.searchsorted(jnp.cumsum(ragged_sizes(part_splits[4], DOCS, PACKED_TOKENS, PACKED_TOKENS // 2, 0)), jnp.arange(PACKED_TOKENS), side="right").astype(jnp.int32),
        "modality": draw_modality(jax.random.fold_in(jax.random.fold_in(arg_keys[9], part), 71), part),
        "input_weights": scatter_about(arg_keys[6], (D, 2, 2 * FF), D ** -0.5, 0.09375, ((2, 16),)),
        "output_weights": scatter_about(arg_keys[7], (2 * FF, D), FF ** -0.5, 0.046875, ((0, 16),)),
        "norm_gains": jnp.clip(1.0 + 0.1 * jax.random.normal(arg_keys[8], (2, D), jnp.float32), 0.5, 1.5),
    }


def swiglu_block(row_block, in_block, out_block):
    unit_count = in_block.shape[2]
    flat_in = in_block.reshape(in_block.shape[0], 2 * unit_count)
    gate_up = jnp.dot(row_block, flat_in, preferred_element_type=jnp.float32)
    activated = (jax.nn.silu(gate_up[:, :unit_count]) * gate_up[:, unit_count:]).astype(jnp.bfloat16)
    return jnp.dot(activated, out_block, preferred_element_type=jnp.float32)

def reference(queries, keys, values, hidden_in, doc_ids, modality, input_weights, output_weights, norm_gains):
    heads_per_group = QUERY_HEADS // KEY_VALUE_HEADS
    positions = jnp.arange(PACKED_TOKENS, dtype=jnp.int32)
    visible = (doc_ids[:, None] == doc_ids[None, :]) & (positions[None, :] <= positions[:, None])
    query_by_group = queries.astype(jnp.float32).reshape(PACKED_TOKENS, KEY_VALUE_HEADS, heads_per_group, HEAD_SIZE)
    key_by_group = keys.astype(jnp.float32).reshape(PACKED_TOKENS, KEY_VALUE_HEADS, HEAD_SIZE)
    value_by_group = values.astype(jnp.float32).reshape(PACKED_TOKENS, KEY_VALUE_HEADS, HEAD_SIZE)
    score_scale = 1.0 / math.sqrt(HEAD_SIZE)

    def single_group(group_index):
        query_part = lax.dynamic_index_in_dim(query_by_group, group_index, 1, keepdims=False)
        key_part = lax.dynamic_index_in_dim(key_by_group, group_index, 1, keepdims=False)
        value_part = lax.dynamic_index_in_dim(value_by_group, group_index, 1, keepdims=False)
        scores = jnp.einsum('tqd,nd->tqn', query_part, key_part, precision=lax.Precision.HIGHEST) * score_scale
        masked = jnp.where(visible[:, None, :], scores, -1e+30)
        row_max = lax.optimization_barrier(jnp.max(masked, axis=-1, keepdims=True))
        weights = jnp.where(visible[:, None, :], jnp.exp(masked - row_max), 0.0)
        total = lax.optimization_barrier(jnp.sum(weights, axis=-1, keepdims=True))
        low_weights = lax.optimization_barrier(weights.astype(jnp.bfloat16)).astype(jnp.float32)
        weighted = jnp.einsum('tqn,nd->tqd', low_weights, value_part, precision=lax.Precision.HIGHEST)
        return weighted / total
    attended_output = lax.map(single_group, jnp.arange(KEY_VALUE_HEADS, dtype=jnp.int32))
    attended_output = jnp.transpose(attended_output, (1, 0, 2, 3)).reshape(PACKED_TOKENS, QUERY_HEADS * HEAD_SIZE)
    residual = (hidden_in.astype(jnp.float32) + attended_output).astype(jnp.bfloat16)
    residual_wide = residual.astype(jnp.float32)
    mean_square = lax.optimization_barrier(jnp.mean(residual_wide * residual_wide, axis=-1, keepdims=True))
    row_gain = jnp.where(modality[:, None] == 1, norm_gains[1][None, :], norm_gains[0][None, :])
    normed = (residual_wide * lax.rsqrt(mean_square + 1e-06) * row_gain).astype(jnp.bfloat16)
    by_modality = jnp.argsort(modality, stable=True)
    sorted_rows = normed[by_modality]
    text_count = PACKED_TOKENS - IMG_ROWS
    text_out = swiglu_block(sorted_rows[:text_count], input_weights[:, :, :FF], output_weights[:FF])
    image_out = swiglu_block(sorted_rows[text_count:], input_weights[:, :, FF:], output_weights[FF:])
    sorted_out = jnp.concatenate([text_out, image_out], axis=0)
    ffn_out = jnp.zeros((PACKED_TOKENS, D), jnp.float32).at[by_modality].set(sorted_out)
    return (residual_wide + ffn_out).astype(jnp.bfloat16)
```

```python
import functools
import math

import jax
import jax.numpy as jnp
from jax import lax
from jax.experimental import pallas as pl
from jax.experimental.pallas import tpu as pltpu
from jax.sharding import PartitionSpec as P

HEAD_SIZE = 128
FF = 18944
CHUNK = 16
NEG = -1e30


def reduce_kernel(
    seq_size, mp_size, part, resid, out,
    pair_recv, cross_send, cross_recv, own, right_send, right_recv, left_send, left_recv,
    pair_s, pair_r, cross_s, cross_r, right_s, right_r, left_s, left_r,
):
    chips = seq_size // 2
    rows = out.shape[0]
    chunks = rows // CHUNK
    me = lax.axis_index("seq")
    z = lax.axis_index("mp")
    core = lax.rem(me, 2)
    chip = lax.div(me, 2)
    partner = chip * 2 + (1 - core)

    def peer(d):
        return lax.rem(chip + d, chips) * 2 + core

    barrier = pltpu.get_barrier_semaphore()
    pl.semaphore_signal(barrier, inc=1, device_id={"seq": partner})
    for d in range(1, chips):
        pl.semaphore_signal(barrier, inc=1, device_id={"seq": peer(d)})

    @pl.when(z > 0)
    def _():
        pl.semaphore_signal(barrier, inc=1, device_id={"mp": z - 1})

    @pl.when(z < mp_size - 1)
    def _():
        pl.semaphore_signal(barrier, inc=1, device_id={"mp": z + 1})

    pl.semaphore_wait(
        barrier, chips + jnp.where(z > 0, 1, 0) + jnp.where(z < mp_size - 1, 1, 0)
    )

    def rows_of(k):
        return pl.ds(k * CHUNK, CHUNK)

    def block_of(seq_index, k):
        return pl.ds(pl.multiple_of(seq_index * rows + k * CHUNK, CHUNK), CHUNK)

    def pair_copy(d, k):
        return pltpu.make_async_remote_copy(
            src_ref=part.at[block_of(lax.rem(chip + d, chips) * 2 + (1 - core), k)],
            dst_ref=pair_recv.at[d, rows_of(k)],
            send_sem=pair_s.at[d, k], recv_sem=pair_r.at[d, k],
            device_id={"seq": partner},
        )

    def cross_copy(d, k):
        return pltpu.make_async_remote_copy(
            src_ref=cross_send.at[d - 1, rows_of(k)],
            dst_ref=cross_recv.at[d - 1, rows_of(k)],
            send_sem=cross_s.at[d - 1, k], recv_sem=cross_r.at[d - 1, k],
            device_id={"seq": peer(d)},
        )

    def right_copy(k):
        return pltpu.make_async_remote_copy(
            src_ref=right_send.at[rows_of(k)], dst_ref=right_recv.at[rows_of(k)],
            send_sem=right_s.at[k], recv_sem=right_r.at[k], device_id={"mp": z + 1},
        )

    def left_copy(k):
        return pltpu.make_async_remote_copy(
            src_ref=left_send.at[rows_of(k)], dst_ref=left_recv.at[rows_of(k)],
            send_sem=left_s.at[k], recv_sem=left_r.at[k], device_id={"mp": z - 1},
        )

    order = list(range(1, chips)) + [0]
    for k in range(chunks):
        for d in order:
            pair_copy(d, k).start()

    @pl.when(z == 0)
    def _():
        right_recv[...] = jnp.zeros_like(right_recv)

    @pl.when(z == mp_size - 1)
    def _():
        left_recv[...] = jnp.zeros_like(left_recv)

    f32 = jnp.float32
    for k in range(chunks):
        for d in range(1, chips):
            pair_copy(d, k).wait_recv()
            mine = part[block_of(peer(d), k), :].astype(f32)
            cross_send[d - 1, rows_of(k)] = (
                mine + pair_recv[d, rows_of(k)].astype(f32)
            ).astype(jnp.bfloat16)
            cross_copy(d, k).start()

    def gather_own(k):
        pair_copy(0, k).wait_recv()
        total = part[block_of(me, k), :].astype(f32) + pair_recv[0, rows_of(k)].astype(f32)
        for d in range(1, chips):
            cross_copy(d, k).wait_recv()
            total = total + cross_recv[d - 1, rows_of(k)].astype(f32)
        own[rows_of(k)] = total

    def step_right(k):
        @pl.when(z > 0)
        def _():
            right_copy(k).wait_recv()

        @pl.when(z < mp_size - 1)
        def _():
            right_send[rows_of(k)] = (
                own[rows_of(k)] + right_recv[rows_of(k)].astype(f32)
            ).astype(jnp.bfloat16)
            right_copy(k).start()

    def step_left(k):
        @pl.when(z < mp_size - 1)
        def _():
            left_copy(k).wait_recv()

        @pl.when(z > 0)
        def _():
            left_send[rows_of(k)] = (
                own[rows_of(k)] + left_recv[rows_of(k)].astype(f32)
            ).astype(jnp.bfloat16)
            left_copy(k).start()

    low_half = z * 2 < mp_size
    for t in range(chunks + 1):
        if t < chunks:
            gather_own(t)

        @pl.when(low_half)
        def _():
            if t < chunks:
                step_right(t)
            if t > 0:
                step_left(t - 1)

        @pl.when(jnp.logical_not(low_half))
        def _():
            if t < chunks:
                step_left(t)
            if t > 0:
                step_right(t - 1)

        if t > 0:
            here = rows_of(t - 1)
            ffn = own[here] + right_recv[here].astype(f32) + left_recv[here].astype(f32)
            out[here] = (resid[here].astype(f32) + ffn).astype(jnp.bfloat16)

    for k in range(chunks):
        for d in range(chips):
            pair_copy(d, k).wait_send()
        for d in range(1, chips):
            cross_copy(d, k).wait_send()

        @pl.when(z < mp_size - 1)
        def _():
            right_copy(k).wait_send()

        @pl.when(z > 0)
        def _():
            left_copy(k).wait_send()


def reduce_rows(part, residual, seq_size, mp_size):
    rows, width = residual.shape
    chips = seq_size // 2
    chunks = rows // CHUNK
    bf16 = jnp.bfloat16
    dma = pltpu.SemaphoreType.DMA
    crossing = max(chips - 1, 1)
    return pl.pallas_call(
        functools.partial(reduce_kernel, seq_size, mp_size),
        out_shape=jax.ShapeDtypeStruct((rows, width), bf16),
        in_specs=[pl.BlockSpec(memory_space=pltpu.VMEM)] * 2,
        out_specs=pl.BlockSpec(memory_space=pltpu.VMEM),
        scratch_shapes=[
            pltpu.VMEM((chips, rows, width), bf16),
            pltpu.VMEM((crossing, rows, width), bf16),
            pltpu.VMEM((crossing, rows, width), bf16),
            pltpu.VMEM((rows, width), jnp.float32),
            pltpu.VMEM((rows, width), bf16),
            pltpu.VMEM((rows, width), bf16),
            pltpu.VMEM((rows, width), bf16),
            pltpu.VMEM((rows, width), bf16),
            dma((chips, chunks)), dma((chips, chunks)),
            dma((crossing, chunks)), dma((crossing, chunks)),
            dma((chunks,)), dma((chunks,)), dma((chunks,)), dma((chunks,)),
        ],
        compiler_params=pltpu.CompilerParams(
            collective_id=1, has_side_effects=True, vmem_limit_bytes=40 * 1024 * 1024
        ),
        name="reduce_rows",
    )(part, residual)


def attend(queries, payload, all_payload, hidden_in, shard_index):
    row_count = queries.shape[0]
    kv_width = (payload.shape[1] - HEAD_SIZE) // 2
    group_count = kv_width // HEAD_SIZE
    head_count = queries.shape[1] // HEAD_SIZE
    total_rows = all_payload.shape[0]
    query_by_group = queries.reshape(
        row_count, group_count, head_count // group_count, HEAD_SIZE
    )
    key_by_group = all_payload[:, :kv_width].reshape(total_rows, group_count, HEAD_SIZE)
    value_by_group = all_payload[:, kv_width : 2 * kv_width].reshape(
        total_rows, group_count, HEAD_SIZE
    )
    scores = jnp.einsum(
        "rgqd,ngd->rgqn", query_by_group, key_by_group, preferred_element_type=jnp.float32
    ) * (1.0 / math.sqrt(HEAD_SIZE))
    position = shard_index * row_count + jnp.arange(row_count, dtype=jnp.int32)
    key_position = jnp.arange(total_rows, dtype=jnp.int32)
    own_doc = payload[:, 2 * kv_width]
    key_doc = all_payload[:, 2 * kv_width]
    visible = (own_doc[:, None] == key_doc[None, :]) & (
        key_position[None, :] <= position[:, None]
    )
    visible = visible[:, None, None, :]
    masked = jnp.where(visible, scores, NEG)
    row_max = jnp.max(masked, axis=-1)
    weights = jnp.where(visible, jnp.exp(masked - row_max[..., None]), 0.0)
    total = jnp.sum(weights, axis=-1)
    weighted = jnp.einsum(
        "rgqn,ngd->rgqd",
        weights.astype(jnp.bfloat16),
        value_by_group,
        preferred_element_type=jnp.float32,
    )
    attended = (weighted / total[..., None]).reshape(row_count, head_count * HEAD_SIZE)
    return (hidden_in.astype(jnp.float32) + attended).astype(jnp.bfloat16)


def normalise(residual, modality, norm_gains):
    wide = residual.astype(jnp.float32)
    mean_square = jnp.mean(wide * wide, axis=-1, keepdims=True)
    gain = jnp.where(modality[:, None] == 1, norm_gains[1][None, :], norm_gains[0][None, :])
    return (wide * lax.rsqrt(mean_square + 1e-06) * gain).astype(jnp.bfloat16)


def feed_forward(all_rows, wanted, input_weights, output_weights):
    unit_count = output_weights.shape[0]
    flat_in = input_weights.reshape(input_weights.shape[0], 2 * unit_count)
    gate_up = jnp.dot(all_rows, flat_in, preferred_element_type=jnp.float32)
    activated = jax.nn.silu(gate_up[:, :unit_count]) * gate_up[:, unit_count:]
    activated = jnp.where(wanted[:, None], activated, 0.0).astype(jnp.bfloat16)
    return jnp.dot(activated, output_weights, preferred_element_type=jnp.float32).astype(
        jnp.bfloat16
    )


def body(
    seq_size, mp_size,
    queries, keys, values, hidden_in, doc_ids, modality, input_weights, output_weights, norm_gains
):
    row_count = queries.shape[0]
    kv_width = keys.shape[1]
    shard_index = lax.axis_index("seq")
    device_index = shard_index * mp_size + lax.axis_index("mp")
    lane = jnp.arange(HEAD_SIZE, dtype=jnp.int32)[None, :]
    tags = jnp.where(lane == 0, doc_ids[:, None], jnp.where(lane == 1, modality[:, None], 0))
    payload = jnp.concatenate([keys, values, tags.astype(jnp.bfloat16)], axis=1)
    all_payload = lax.all_gather(payload, "seq", axis=0, tiled=True)
    residual = attend(queries, payload, all_payload, hidden_in, shard_index)
    normed = normalise(residual, modality, norm_gains)
    all_rows = lax.all_gather(normed, "seq", axis=0, tiled=True)
    is_image = device_index >= FF // output_weights.shape[0]
    wanted = (all_payload[:, 2 * kv_width + 1] > 0.5) == is_image
    part = feed_forward(all_rows, wanted, input_weights, output_weights)
    return reduce_rows(part, residual, seq_size, mp_size)


def solution(mesh):
    rows_spec = P(("groups", "seq"), None)
    in_specs = (
        rows_spec, rows_spec, rows_spec, rows_spec,
        P(("groups", "seq")), P(("groups", "seq")),
        P(None, None, ("seq", "mp")), P(("seq", "mp"), None), P(),
    )
    f = functools.partial(body, mesh.shape["seq"], mesh.shape["mp"])
    return jax.shard_map(f, mesh=mesh, in_specs=in_specs, out_specs=rows_spec, check_vma=False)
```

```python
import functools
import math

import jax
import jax.numpy as jnp
from jax import lax
from jax.experimental import pallas as pl
from jax.experimental.pallas import tpu as pltpu
from jax.sharding import PartitionSpec as P

HEAD_SIZE = 128
FF = 18944
CHUNK = 16
COLS = 512
UNIT_TILE = 256
ROW_TILE = 256
SLOTS = 6
LAG = 2
NEG = -1e30


def split_units(units):
    if units % 16:
        return [(0, units)]
    return [(o, min(UNIT_TILE, units - o)) for o in range(0, units, UNIT_TILE)]


def ffn_kernel(
    seq_size, mp_size, normed, resid, wanted, w_in, w_out, out,
    x, ring, w_down, act, part,
    pair_recv, cross_send, cross_recv, own, right_send, right_recv, left_send, left_recv,
    near_s, near_r, far_s, far_r, relay_s, relay_r, keep_sem, ring_sem, down_sem,
    pair_s, pair_r, cross_s, cross_r, right_s, right_r, left_s, left_r,
):
    chips = seq_size // 2
    rows, width = out.shape
    chunks = width // COLS
    total_rows = x.shape[0]
    units = w_down.shape[0]
    tiles = split_units(units)
    slots = ring.shape[0]
    f32 = jnp.float32
    me = lax.axis_index("seq")
    z = lax.axis_index("mp")
    core = lax.rem(me, 2)
    chip = lax.div(me, 2)
    partner = chip * 2 + (1 - core)

    def peer(d):
        return lax.rem(chip + d, chips) * 2 + core

    def source(d):
        return lax.rem(chip + chips - d, chips) * 2 + core

    def load(t):
        offset, size = tiles[t]
        return pltpu.make_async_copy(
            w_in.at[:, pl.ds(offset, size)],
            ring.at[t % slots, :, pl.ds(0, size)],
            ring_sem.at[t],
        )

    down_load = pltpu.make_async_copy(w_out, w_down, down_sem)
    for t in range(min(slots, len(tiles))):
        load(t).start()
    down_load.start()

    barrier = pltpu.get_barrier_semaphore()
    pl.semaphore_signal(barrier, inc=1, device_id={"seq": partner})
    for d in range(1, chips):
        pl.semaphore_signal(barrier, inc=1, device_id={"seq": peer(d)})

    @pl.when(z > 0)
    def _():
        pl.semaphore_signal(barrier, inc=1, device_id={"mp": z - 1})

    @pl.when(z < mp_size - 1)
    def _():
        pl.semaphore_signal(barrier, inc=1, device_id={"mp": z + 1})

    pl.semaphore_wait(
        barrier, chips + jnp.where(z > 0, 1, 0) + jnp.where(z < mp_size - 1, 1, 0)
    )

    row_chunks = rows // CHUNK

    def place(seq_index, k):
        return x.at[pl.ds(pl.multiple_of(seq_index * rows + k * CHUNK, CHUNK), CHUNK)]

    def near_copy(k):
        return pltpu.make_async_remote_copy(
            src_ref=normed.at[pl.ds(k * CHUNK, CHUNK)], dst_ref=place(me, k),
            send_sem=near_s.at[k], recv_sem=near_r.at[k], device_id={"seq": partner},
        )

    def far_copy(d, k):
        return pltpu.make_async_remote_copy(
            src_ref=normed.at[pl.ds(k * CHUNK, CHUNK)], dst_ref=place(me, k),
            send_sem=far_s.at[d - 1, k], recv_sem=far_r.at[d - 1, k],
            device_id={"seq": peer(d)},
        )

    def relay_copy(d, k):
        return pltpu.make_async_remote_copy(
            src_ref=place(source(d), k), dst_ref=place(source(d), k),
            send_sem=relay_s.at[d - 1, k], recv_sem=relay_r.at[d - 1, k],
            device_id={"seq": partner},
        )

    keep = pltpu.make_async_copy(
        normed, x.at[pl.ds(pl.multiple_of(me * rows, rows), rows)], keep_sem
    )
    for k in range(row_chunks):
        for d in range(1, chips):
            far_copy(d, k).start()
    for k in range(row_chunks):
        near_copy(k).start()
    keep.start()

    @pl.when(z == 0)
    def _():
        right_recv[...] = jnp.zeros_like(right_recv)

    @pl.when(z == mp_size - 1)
    def _():
        left_recv[...] = jnp.zeros_like(left_recv)

    for k in range(row_chunks):
        for d in range(1, chips):
            far_copy(d, k).wait_recv()
            relay_copy(d, k).start()
    keep.wait()
    for k in range(row_chunks):
        near_copy(k).wait()
        for d in range(1, chips):
            far_copy(d, k).wait_send()
            relay_copy(d, k).wait()

    blocks = total_rows // ROW_TILE if total_rows % ROW_TILE == 0 else 1
    block_rows = total_rows // blocks
    last_dims = (((1,), (1,)), ((), ()))

    def rows_at(i):
        return pl.ds(pl.multiple_of(i * block_rows, block_rows), block_rows)

    for t, (offset, size) in enumerate(tiles):
        load(t).wait()
        slot = t % slots

        def gate_up(i, carry, slot=slot, offset=offset, size=size):
            here = x[rows_at(i), :]
            gate = lax.dot_general(
                here, ring[slot, 0, :size, :], last_dims, preferred_element_type=f32
            )
            up = lax.dot_general(
                here, ring[slot, 1, :size, :], last_dims, preferred_element_type=f32
            )
            value = gate / (1.0 + jnp.exp(-gate)) * up
            value = jnp.where(wanted[rows_at(i), :1] > 0.5, value, 0.0)
            act[rows_at(i), pl.ds(offset, size)] = value.astype(jnp.bfloat16)
            return carry

        lax.fori_loop(0, blocks, gate_up, 0)
        if t + slots < len(tiles):
            load(t + slots).start()
    down_load.wait()

    def cols(k):
        return pl.ds(k * COLS, COLS)

    def block_of(seq_index):
        return pl.ds(pl.multiple_of(seq_index * rows, rows), rows)

    def pair_copy(d, k):
        return pltpu.make_async_remote_copy(
            src_ref=part.at[k, block_of(lax.rem(chip + d, chips) * 2 + (1 - core))],
            dst_ref=pair_recv.at[k, d],
            send_sem=pair_s.at[d, k], recv_sem=pair_r.at[d, k],
            device_id={"seq": partner},
        )

    def cross_copy(d, k):
        return pltpu.make_async_remote_copy(
            src_ref=cross_send.at[k, d - 1], dst_ref=cross_recv.at[k, d - 1],
            send_sem=cross_s.at[d - 1, k], recv_sem=cross_r.at[d - 1, k],
            device_id={"seq": peer(d)},
        )

    def right_copy(k):
        return pltpu.make_async_remote_copy(
            src_ref=right_send.at[k], dst_ref=right_recv.at[k],
            send_sem=right_s.at[k], recv_sem=right_r.at[k], device_id={"mp": z + 1},
        )

    def left_copy(k):
        return pltpu.make_async_remote_copy(
            src_ref=left_send.at[k], dst_ref=left_recv.at[k],
            send_sem=left_s.at[k], recv_sem=left_r.at[k], device_id={"mp": z - 1},
        )

    def cross_stage(k):
        for d in range(1, chips):
            pair_copy(d, k).wait_recv()
            cross_send[k, d - 1] = (
                part[k, block_of(peer(d)), :].astype(f32) + pair_recv[k, d].astype(f32)
            ).astype(jnp.bfloat16)
            cross_copy(d, k).start()

    order = list(range(1, chips)) + [0]
    for k in range(chunks):

        def down(i, carry, k=k):
            part[k, rows_at(i), :] = jnp.dot(
                act[rows_at(i), :], w_down[:, cols(k)], preferred_element_type=f32
            ).astype(jnp.bfloat16)
            return carry

        lax.fori_loop(0, blocks, down, 0)
        for d in order:
            pair_copy(d, k).start()
        if k > 0:
            cross_stage(k - 1)
    cross_stage(chunks - 1)

    def gather_own(k):
        pair_copy(0, k).wait_recv()
        total = part[k, block_of(me), :].astype(f32) + pair_recv[k, 0].astype(f32)
        for d in range(1, chips):
            cross_copy(d, k).wait_recv()
            total = total + cross_recv[k, d - 1].astype(f32)
        own[k] = total

    def step_right(k):
        @pl.when(z > 0)
        def _():
            right_copy(k).wait_recv()

        @pl.when(z < mp_size - 1)
        def _():
            right_send[k] = (own[k] + right_recv[k].astype(f32)).astype(jnp.bfloat16)
            right_copy(k).start()

    def step_left(k):
        @pl.when(z < mp_size - 1)
        def _():
            left_copy(k).wait_recv()

        @pl.when(z > 0)
        def _():
            left_send[k] = (own[k] + left_recv[k].astype(f32)).astype(jnp.bfloat16)
            left_copy(k).start()

    low_half = z * 2 < mp_size
    for t in range(chunks + LAG):
        if t < chunks:
            gather_own(t)

        @pl.when(low_half)
        def _():
            if t < chunks:
                step_right(t)
            if t >= LAG:
                step_left(t - LAG)

        @pl.when(jnp.logical_not(low_half))
        def _():
            if t < chunks:
                step_left(t)
            if t >= LAG:
                step_right(t - LAG)

        if t >= LAG:
            k = t - LAG
            ffn = own[k] + right_recv[k].astype(f32) + left_recv[k].astype(f32)
            out[:, cols(k)] = (resid[:, cols(k)].astype(f32) + ffn).astype(jnp.bfloat16)

    for k in range(chunks):
        for d in range(chips):
            pair_copy(d, k).wait_send()
        for d in range(1, chips):
            cross_copy(d, k).wait_send()

        @pl.when(z < mp_size - 1)
        def _():
            right_copy(k).wait_send()

        @pl.when(z > 0)
        def _():
            left_copy(k).wait_send()


def feed_forward(normed, residual, wanted, input_weights, output_weights, seq_size, mp_size):
    rows, width = residual.shape
    total_rows = rows * seq_size
    units = output_weights.shape[0]
    chips = seq_size // 2
    chunks = width // COLS
    row_chunks = rows // CHUNK
    bf16 = jnp.bfloat16
    dma = pltpu.SemaphoreType.DMA
    crossing = max(chips - 1, 1)
    tiles = split_units(units)
    slots = min(SLOTS, len(tiles))
    flops = 6 * total_rows * width * units
    vmem = pl.BlockSpec(memory_space=pltpu.VMEM)
    hbm = pl.BlockSpec(memory_space=pl.ANY)
    return pl.pallas_call(
        functools.partial(ffn_kernel, seq_size, mp_size),
        out_shape=jax.ShapeDtypeStruct((rows, width), bf16),
        in_specs=[vmem, vmem, vmem, hbm, hbm],
        out_specs=vmem,
        scratch_shapes=[
            pltpu.VMEM((total_rows, width), bf16),
            pltpu.VMEM((slots, 2, tiles[0][1], width), bf16),
            pltpu.VMEM((units, width), bf16),
            pltpu.VMEM((total_rows, units), bf16),
            pltpu.VMEM((chunks, total_rows, COLS), bf16),
            pltpu.VMEM((chunks, chips, rows, COLS), bf16),
            pltpu.VMEM((chunks, crossing, rows, COLS), bf16),
            pltpu.VMEM((chunks, crossing, rows, COLS), bf16),
            pltpu.VMEM((chunks, rows, COLS), jnp.float32),
            pltpu.VMEM((chunks, rows, COLS), bf16),
            pltpu.VMEM((chunks, rows, COLS), bf16),
            pltpu.VMEM((chunks, rows, COLS), bf16),
            pltpu.VMEM((chunks, rows, COLS), bf16),
            dma((row_chunks,)), dma((row_chunks,)),
            dma((crossing, row_chunks)), dma((crossing, row_chunks)),
            dma((crossing, row_chunks)), dma((crossing, row_chunks)),
            dma(()), dma((len(tiles),)), dma(()),
            dma((chips, chunks)), dma((chips, chunks)),
            dma((crossing, chunks)), dma((crossing, chunks)),
            dma((chunks,)), dma((chunks,)), dma((chunks,)), dma((chunks,)),
        ],
        compiler_params=pltpu.CompilerParams(
            collective_id=1, has_side_effects=True, vmem_limit_bytes=58 * 1024 * 1024
        ),
        cost_estimate=pl.CostEstimate(
            flops=flops, bytes_accessed=6 * units * width, transcendentals=0
        ),
        name="feed_forward",
    )(normed, residual, wanted, input_weights, output_weights)


def attend(queries, payload, all_payload, hidden_in, shard_index):
    row_count = queries.shape[0]
    kv_width = (payload.shape[1] - HEAD_SIZE) // 2
    group_count = kv_width // HEAD_SIZE
    head_count = queries.shape[1] // HEAD_SIZE
    total_rows = all_payload.shape[0]
    query_by_group = queries.reshape(
        row_count, group_count, head_count // group_count, HEAD_SIZE
    )
    key_by_group = all_payload[:, :kv_width].reshape(total_rows, group_count, HEAD_SIZE)
    value_by_group = all_payload[:, kv_width : 2 * kv_width].reshape(
        total_rows, group_count, HEAD_SIZE
    )
    scores = jnp.einsum(
        "rgqd,ngd->rgqn", query_by_group, key_by_group, preferred_element_type=jnp.float32
    ) * (1.0 / math.sqrt(HEAD_SIZE))
    position = shard_index * row_count + jnp.arange(row_count, dtype=jnp.int32)
    key_position = jnp.arange(total_rows, dtype=jnp.int32)
    own_doc = payload[:, 2 * kv_width]
    key_doc = all_payload[:, 2 * kv_width]
    visible = (own_doc[:, None] == key_doc[None, :]) & (
        key_position[None, :] <= position[:, None]
    )
    visible = visible[:, None, None, :]
    masked = jnp.where(visible, scores, NEG)
    row_max = jnp.max(masked, axis=-1)
    weights = jnp.where(visible, jnp.exp(masked - row_max[..., None]), 0.0)
    total = jnp.sum(weights, axis=-1)
    weighted = jnp.einsum(
        "rgqn,ngd->rgqd",
        weights.astype(jnp.bfloat16),
        value_by_group,
        preferred_element_type=jnp.float32,
    )
    attended = (weighted / total[..., None]).reshape(row_count, head_count * HEAD_SIZE)
    return (hidden_in.astype(jnp.float32) + attended).astype(jnp.bfloat16)


def normalise(residual, modality, norm_gains):
    wide = residual.astype(jnp.float32)
    mean_square = jnp.mean(wide * wide, axis=-1, keepdims=True)
    gain = jnp.where(modality[:, None] == 1, norm_gains[1][None, :], norm_gains[0][None, :])
    return (wide * lax.rsqrt(mean_square + 1e-06) * gain).astype(jnp.bfloat16)


def body(
    seq_size, mp_size,
    queries, keys, values, hidden_in, doc_ids, modality, input_weights, output_weights, norm_gains
):
    row_count = queries.shape[0]
    kv_width = keys.shape[1]
    shard_index = lax.axis_index("seq")
    device_index = shard_index * mp_size + lax.axis_index("mp")
    lane = jnp.arange(HEAD_SIZE, dtype=jnp.int32)[None, :]
    tags = jnp.where(lane == 0, doc_ids[:, None], jnp.where(lane == 1, modality[:, None], 0))
    payload = jnp.concatenate([keys, values, tags.astype(jnp.bfloat16)], axis=1)
    all_payload = lax.all_gather(payload, "seq", axis=0, tiled=True)
    residual = attend(queries, payload, all_payload, hidden_in, shard_index)
    normed = normalise(residual, modality, norm_gains)
    is_image = device_index >= FF // output_weights.shape[0]
    wanted = (all_payload[:, 2 * kv_width + 1] > 0.5) == is_image
    wanted = jnp.broadcast_to(wanted[:, None], (wanted.shape[0], HEAD_SIZE)).astype(jnp.float32)
    by_unit = jnp.transpose(input_weights, (1, 2, 0))
    return feed_forward(
        normed, residual, wanted, by_unit, output_weights, seq_size, mp_size
    )


def solution(mesh):
    rows_spec = P(("groups", "seq"), None)
    in_specs = (
        rows_spec, rows_spec, rows_spec, rows_spec,
        P(("groups", "seq")), P(("groups", "seq")),
        P(None, None, ("seq", "mp")), P(("seq", "mp"), None), P(),
    )
    f = functools.partial(body, mesh.shape["seq"], mesh.shape["mp"])
    return jax.shard_map(f, mesh=mesh, in_specs=in_specs, out_specs=rows_spec, check_vma=False)
```

```python
import functools
import math

import jax
import jax.numpy as jnp
from jax import lax
from jax.experimental import pallas as pl
from jax.experimental.pallas import tpu as pltpu
from jax.sharding import PartitionSpec as P

HEAD_SIZE = 128
FF = 18944
CHUNK = 16
COLS = 512
UNIT_TILE = 256
ROW_TILE = 256
SLOTS = 6
LAG = 2
NEG = -1e30


def split_units(units):
    if units % 16:
        return [(0, units)]
    return [(o, min(UNIT_TILE, units - o)) for o in range(0, units, UNIT_TILE)]


def ffn_kernel(
    seq_size, mp_size, queries, keys, values, tags, hidden, gains, w_in, w_out, out,
    kv, resid, normed, kv_s, kv_r,
    x, ring, w_down, act, part,
    pair_recv, cross_send, cross_recv, own, right_send, right_recv, left_send, left_recv,
    near_s, near_r, far_s, far_r, relay_s, relay_r, keep_sem, ring_sem, down_sem,
    pair_s, pair_r, cross_s, cross_r, right_s, right_r, left_s, left_r,
):
    chips = seq_size // 2
    rows, width = out.shape
    chunks = width // COLS
    total_rows = x.shape[0]
    units = w_down.shape[0]
    tiles = split_units(units)
    slots = ring.shape[0]
    f32 = jnp.float32
    me = lax.axis_index("seq")
    z = lax.axis_index("mp")
    core = lax.rem(me, 2)
    chip = lax.div(me, 2)
    partner = chip * 2 + (1 - core)

    def peer(d):
        return lax.rem(chip + d, chips) * 2 + core

    def source(d):
        return lax.rem(chip + chips - d, chips) * 2 + core

    def load(t):
        offset, size = tiles[t]
        return pltpu.make_async_copy(
            w_in.at[:, pl.ds(offset, size)],
            ring.at[t % slots, :, pl.ds(0, size)],
            ring_sem.at[t],
        )

    down_load = pltpu.make_async_copy(w_out, w_down, down_sem)
    for t in range(min(slots, len(tiles))):
        load(t).start()
    down_load.start()

    barrier = pltpu.get_barrier_semaphore()
    for d in range(1, seq_size):
        pl.semaphore_signal(barrier, inc=1, device_id={"seq": lax.rem(me + d, seq_size)})

    @pl.when(z > 0)
    def _():
        pl.semaphore_signal(barrier, inc=1, device_id={"mp": z - 1})

    @pl.when(z < mp_size - 1)
    def _():
        pl.semaphore_signal(barrier, inc=1, device_id={"mp": z + 1})

    pl.semaphore_wait(
        barrier, seq_size - 1 + jnp.where(z > 0, 1, 0) + jnp.where(z < mp_size - 1, 1, 0)
    )

    kv_width = keys.shape[1]
    group_count = kv_width // HEAD_SIZE
    heads = width // HEAD_SIZE // group_count
    own_rows = pl.ds(pl.multiple_of(me * rows, rows), rows)
    pieces = ((keys, 0, kv_width), (values, kv_width, kv_width), (tags, 2 * kv_width, HEAD_SIZE))

    def kv_copy(d, p):
        ref, offset, size = pieces[p]
        return pltpu.make_async_remote_copy(
            src_ref=ref, dst_ref=kv.at[own_rows, pl.ds(offset, size)],
            send_sem=kv_s.at[d - 1, p], recv_sem=kv_r.at[d - 1, p],
            device_id={"seq": lax.rem(me + d, seq_size)},
        )

    for d in range(1, seq_size):
        for p in range(3):
            kv_copy(d, p).start()
    for ref, offset, size in pieces:
        kv[own_rows, pl.ds(offset, size)] = ref[...]
    for d in range(1, seq_size):
        for p in range(3):
            kv_copy(d, p).wait()

    lane = lax.broadcasted_iota(jnp.int32, (rows, HEAD_SIZE), 1)
    own_tags = tags[...].astype(f32)
    own_docs = jnp.where(lane < HEAD_SIZE // 2, own_tags, 0.0).astype(jnp.bfloat16)
    nt = (((1,), (1,)), ((), ()))
    same = lax.dot_general(
        own_docs, kv[:, 2 * kv_width :], nt, preferred_element_type=f32
    )
    position = me * rows + lax.broadcasted_iota(jnp.int32, same.shape, 0)
    key_position = lax.broadcasted_iota(jnp.int32, same.shape, 1)
    same = jnp.where(key_position <= position, same, 0.0)
    visible = jnp.concatenate([same] * heads, axis=0) > 0.5
    square = jnp.zeros((rows, 1), f32)
    for g in range(group_count):
        first = g * heads * HEAD_SIZE
        stacked = jnp.concatenate(
            [queries[:, first + h * HEAD_SIZE : first + (h + 1) * HEAD_SIZE] for h in range(heads)],
            axis=0,
        )
        scores = lax.dot_general(
            stacked, kv[:, g * HEAD_SIZE : (g + 1) * HEAD_SIZE], nt, preferred_element_type=f32
        ) * (1.0 / math.sqrt(HEAD_SIZE))
        masked = jnp.where(visible, scores, NEG)
        top = jnp.max(masked, axis=1, keepdims=True)
        weights = jnp.where(visible, jnp.exp(masked - top), 0.0)
        total = jnp.sum(weights, axis=1, keepdims=True)
        attended = jnp.dot(
            weights.astype(jnp.bfloat16),
            kv[:, kv_width + g * HEAD_SIZE : kv_width + (g + 1) * HEAD_SIZE],
            preferred_element_type=f32,
        ) / total
        for h in range(heads):
            part_cols = pl.ds(first + h * HEAD_SIZE, HEAD_SIZE)
            low = (
                hidden[:, part_cols].astype(f32) + attended[h * rows : (h + 1) * rows]
            ).astype(jnp.bfloat16)
            resid[:, part_cols] = low
            wide = low.astype(f32)
            square = square + jnp.sum(wide * wide, axis=1, keepdims=True)
    scale = lax.rsqrt(square * (1.0 / width) + 1e-06)
    image_row = own_tags[:, HEAD_SIZE - 1 :] > 0.5
    for c in range(width // COLS):
        part_cols = pl.ds(c * COLS, COLS)
        gain = jnp.where(image_row, gains[1:2, part_cols], gains[0:1, part_cols])
        normed[:, part_cols] = (
            resid[:, part_cols].astype(f32) * scale * gain
        ).astype(jnp.bfloat16)

    target = jnp.where(me * mp_size + z >= FF // units, 1.0, 0.0)
    row_chunks = rows // CHUNK

    def place(seq_index, k):
        return x.at[pl.ds(pl.multiple_of(seq_index * rows + k * CHUNK, CHUNK), CHUNK)]

    def near_copy(k):
        return pltpu.make_async_remote_copy(
            src_ref=normed.at[pl.ds(k * CHUNK, CHUNK)], dst_ref=place(me, k),
            send_sem=near_s.at[k], recv_sem=near_r.at[k], device_id={"seq": partner},
        )

    def far_copy(d, k):
        return pltpu.make_async_remote_copy(
            src_ref=normed.at[pl.ds(k * CHUNK, CHUNK)], dst_ref=place(me, k),
            send_sem=far_s.at[d - 1, k], recv_sem=far_r.at[d - 1, k],
            device_id={"seq": peer(d)},
        )

    def relay_copy(d, k):
        return pltpu.make_async_remote_copy(
            src_ref=place(source(d), k), dst_ref=place(source(d), k),
            send_sem=relay_s.at[d - 1, k], recv_sem=relay_r.at[d - 1, k],
            device_id={"seq": partner},
        )

    keep = pltpu.make_async_copy(
        normed, x.at[pl.ds(pl.multiple_of(me * rows, rows), rows)], keep_sem
    )
    for k in range(row_chunks):
        for d in range(1, chips):
            far_copy(d, k).start()
    for k in range(row_chunks):
        near_copy(k).start()
    keep.start()

    @pl.when(z == 0)
    def _():
        right_recv[...] = jnp.zeros_like(right_recv)

    @pl.when(z == mp_size - 1)
    def _():
        left_recv[...] = jnp.zeros_like(left_recv)

    for k in range(row_chunks):
        for d in range(1, chips):
            far_copy(d, k).wait_recv()
            relay_copy(d, k).start()
    keep.wait()
    for k in range(row_chunks):
        near_copy(k).wait()
        for d in range(1, chips):
            far_copy(d, k).wait_send()
            relay_copy(d, k).wait()

    blocks = total_rows // ROW_TILE if total_rows % ROW_TILE == 0 else 1
    block_rows = total_rows // blocks
    last_dims = (((1,), (1,)), ((), ()))

    def rows_at(i):
        return pl.ds(pl.multiple_of(i * block_rows, block_rows), block_rows)

    for t, (offset, size) in enumerate(tiles):
        load(t).wait()
        slot = t % slots

        def gate_up(i, carry, slot=slot, offset=offset, size=size):
            here = x[rows_at(i), :]
            gate = lax.dot_general(
                here, ring[slot, 0, :size, :], last_dims, preferred_element_type=f32
            )
            up = lax.dot_general(
                here, ring[slot, 1, :size, :], last_dims, preferred_element_type=f32
            )
            value = gate / (1.0 + jnp.exp(-gate)) * up
            value = jnp.where(
                jnp.abs(kv[rows_at(i), kv.shape[1] - 1 :].astype(f32) - target) < 0.5, value, 0.0
            )
            act[rows_at(i), pl.ds(offset, size)] = value.astype(jnp.bfloat16)
            return carry

        lax.fori_loop(0, blocks, gate_up, 0)
        if t + slots < len(tiles):
            load(t + slots).start()
    down_load.wait()

    def cols(k):
        return pl.ds(k * COLS, COLS)

    def block_of(seq_index):
        return pl.ds(pl.multiple_of(seq_index * rows, rows), rows)

    def pair_copy(d, k):
        return pltpu.make_async_remote_copy(
            src_ref=part.at[k, block_of(lax.rem(chip + d, chips) * 2 + (1 - core))],
            dst_ref=pair_recv.at[k, d],
            send_sem=pair_s.at[d, k], recv_sem=pair_r.at[d, k],
            device_id={"seq": partner},
        )

    def cross_copy(d, k):
        return pltpu.make_async_remote_copy(
            src_ref=cross_send.at[k, d - 1], dst_ref=cross_recv.at[k, d - 1],
            send_sem=cross_s.at[d - 1, k], recv_sem=cross_r.at[d - 1, k],
            device_id={"seq": peer(d)},
        )

    def right_copy(k):
        return pltpu.make_async_remote_copy(
            src_ref=right_send.at[k], dst_ref=right_recv.at[k],
            send_sem=right_s.at[k], recv_sem=right_r.at[k], device_id={"mp": z + 1},
        )

    def left_copy(k):
        return pltpu.make_async_remote_copy(
            src_ref=left_send.at[k], dst_ref=left_recv.at[k],
            send_sem=left_s.at[k], recv_sem=left_r.at[k], device_id={"mp": z - 1},
        )

    def cross_stage(k):
        for d in range(1, chips):
            pair_copy(d, k).wait_recv()
            cross_send[k, d - 1] = (
                part[k, block_of(peer(d)), :].astype(f32) + pair_recv[k, d].astype(f32)
            ).astype(jnp.bfloat16)
            cross_copy(d, k).start()

    order = list(range(1, chips)) + [0]
    for k in range(chunks):

        def down(i, carry, k=k):
            part[k, rows_at(i), :] = jnp.dot(
                act[rows_at(i), :], w_down[:, cols(k)], preferred_element_type=f32
            ).astype(jnp.bfloat16)
            return carry

        lax.fori_loop(0, blocks, down, 0)
        for d in order:
            pair_copy(d, k).start()
        if k > 0:
            cross_stage(k - 1)
    cross_stage(chunks - 1)

    def gather_own(k):
        pair_copy(0, k).wait_recv()
        total = part[k, block_of(me), :].astype(f32) + pair_recv[k, 0].astype(f32)
        for d in range(1, chips):
            cross_copy(d, k).wait_recv()
            total = total + cross_recv[k, d - 1].astype(f32)
        own[k] = total

    def step_right(k):
        @pl.when(z > 0)
        def _():
            right_copy(k).wait_recv()

        @pl.when(z < mp_size - 1)
        def _():
            right_send[k] = (own[k] + right_recv[k].astype(f32)).astype(jnp.bfloat16)
            right_copy(k).start()

    def step_left(k):
        @pl.when(z < mp_size - 1)
        def _():
            left_copy(k).wait_recv()

        @pl.when(z > 0)
        def _():
            left_send[k] = (own[k] + left_recv[k].astype(f32)).astype(jnp.bfloat16)
            left_copy(k).start()

    low_half = z * 2 < mp_size
    for t in range(chunks + LAG):
        if t < chunks:
            gather_own(t)

        @pl.when(low_half)
        def _():
            if t < chunks:
                step_right(t)
            if t >= LAG:
                step_left(t - LAG)

        @pl.when(jnp.logical_not(low_half))
        def _():
            if t < chunks:
                step_left(t)
            if t >= LAG:
                step_right(t - LAG)

        if t >= LAG:
            k = t - LAG
            ffn = own[k] + right_recv[k].astype(f32) + left_recv[k].astype(f32)
            out[:, cols(k)] = (resid[:, cols(k)].astype(f32) + ffn).astype(jnp.bfloat16)

    for k in range(chunks):
        for d in range(chips):
            pair_copy(d, k).wait_send()
        for d in range(1, chips):
            cross_copy(d, k).wait_send()

        @pl.when(z < mp_size - 1)
        def _():
            right_copy(k).wait_send()

        @pl.when(z > 0)
        def _():
            left_copy(k).wait_send()


def layer(
    queries, keys, values, tags, hidden, gains, input_weights, output_weights, seq_size, mp_size
):
    rows, width = queries.shape
    total_rows = rows * seq_size
    units = output_weights.shape[0]
    chips = seq_size // 2
    chunks = width // COLS
    row_chunks = rows // CHUNK
    bf16 = jnp.bfloat16
    dma = pltpu.SemaphoreType.DMA
    crossing = max(chips - 1, 1)
    tiles = split_units(units)
    slots = min(SLOTS, len(tiles))
    flops = 6 * total_rows * width * units
    vmem = pl.BlockSpec(memory_space=pltpu.VMEM)
    hbm = pl.BlockSpec(memory_space=pl.ANY)
    return pl.pallas_call(
        functools.partial(ffn_kernel, seq_size, mp_size),
        out_shape=jax.ShapeDtypeStruct((rows, width), bf16),
        in_specs=[vmem] * 6 + [hbm, hbm],
        out_specs=vmem,
        scratch_shapes=[
            pltpu.VMEM((total_rows, 2 * keys.shape[1] + HEAD_SIZE), bf16),
            pltpu.VMEM((rows, width), bf16),
            pltpu.VMEM((rows, width), bf16),
            dma((seq_size - 1, 3)), dma((seq_size - 1, 3)),
            pltpu.VMEM((total_rows, width), bf16),
            pltpu.VMEM((slots, 2, tiles[0][1], width), bf16),
            pltpu.VMEM((units, width), bf16),
            pltpu.VMEM((total_rows, units), bf16),
            pltpu.VMEM((chunks, total_rows, COLS), bf16),
            pltpu.VMEM((chunks, chips, rows, COLS), bf16),
            pltpu.VMEM((chunks, crossing, rows, COLS), bf16),
            pltpu.VMEM((chunks, crossing, rows, COLS), bf16),
            pltpu.VMEM((chunks, rows, COLS), jnp.float32),
            pltpu.VMEM((chunks, rows, COLS), bf16),
            pltpu.VMEM((chunks, rows, COLS), bf16),
            pltpu.VMEM((chunks, rows, COLS), bf16),
            pltpu.VMEM((chunks, rows, COLS), bf16),
            dma((row_chunks,)), dma((row_chunks,)),
            dma((crossing, row_chunks)), dma((crossing, row_chunks)),
            dma((crossing, row_chunks)), dma((crossing, row_chunks)),
            dma(()), dma((len(tiles),)), dma(()),
            dma((chips, chunks)), dma((chips, chunks)),
            dma((crossing, chunks)), dma((crossing, chunks)),
            dma((chunks,)), dma((chunks,)), dma((chunks,)), dma((chunks,)),
        ],
        compiler_params=pltpu.CompilerParams(
            collective_id=1, has_side_effects=True, vmem_limit_bytes=58 * 1024 * 1024
        ),
        cost_estimate=pl.CostEstimate(
            flops=flops, bytes_accessed=6 * units * width, transcendentals=0
        ),
        name="layer",
    )(queries, keys, values, tags, hidden, gains, input_weights, output_weights)


def body(
    seq_size, mp_size,
    queries, keys, values, hidden_in, doc_ids, modality, input_weights, output_weights, norm_gains
):
    lane = jnp.arange(HEAD_SIZE, dtype=jnp.int32)[None, :]
    tags = jnp.where(
        lane < HEAD_SIZE // 2, lane == doc_ids[:, None], modality[:, None] == 1
    ).astype(jnp.bfloat16)
    by_unit = jnp.transpose(input_weights, (1, 2, 0))
    return layer(
        queries, keys, values, tags, hidden_in, norm_gains, by_unit, output_weights,
        seq_size, mp_size,
    )


def solution(mesh):
    rows_spec = P(("groups", "seq"), None)
    in_specs = (
        rows_spec, rows_spec, rows_spec, rows_spec,
        P(("groups", "seq")), P(("groups", "seq")),
        P(None, None, ("seq", "mp")), P(("seq", "mp"), None), P(),
    )
    f = functools.partial(body, mesh.shape["seq"], mesh.shape["mp"])
    return jax.shard_map(f, mesh=mesh, in_specs=in_specs, out_specs=rows_spec, check_vma=False)
```

```python
import functools
import math

import jax
import jax.numpy as jnp
from jax import lax
from jax.experimental import pallas as pl
from jax.experimental.pallas import tpu as pltpu
from jax.sharding import PartitionSpec as P

HEAD_SIZE = 128
FF = 18944
CHUNK = 16
COLS = 512
UNIT_TILE = 256
ROW_TILE = 256
SLOTS = 6
LAG = 2
SKEW = 3
NEG = -1e30


def split_units(units):
    if units % 16:
        return [(0, units)]
    return [(o, min(UNIT_TILE, units - o)) for o in range(0, units, UNIT_TILE)]


def ffn_kernel(
    seq_size, mp_size, queries, keys, values, tags, hidden, gains, w_in, w_out, out,
    kv, resid, normed, kv_s, kv_r,
    x, ring, w_down, act, part,
    pair_recv, cross_send, cross_recv, own, right_send, right_recv, left_send, left_recv,
    near_s, near_r, far_s, far_r, relay_s, relay_r, keep_sem, ring_sem, down_sem,
    pair_s, pair_r, cross_s, cross_r, right_s, right_r, left_s, left_r,
):
    chips = seq_size // 2
    rows, width = out.shape
    chunks = width // COLS
    total_rows = x.shape[0]
    units = w_down.shape[0]
    tiles = split_units(units)
    slots = ring.shape[0]
    f32 = jnp.float32
    me = lax.axis_index("seq")
    z = lax.axis_index("mp")
    core = lax.rem(me, 2)
    chip = lax.div(me, 2)
    partner = chip * 2 + (1 - core)

    def peer(d):
        return lax.rem(chip + d, chips) * 2 + core

    def source(d):
        return lax.rem(chip + chips - d, chips) * 2 + core

    def load(t):
        offset, size = tiles[t]
        return pltpu.make_async_copy(
            w_in.at[:, pl.ds(offset, size)],
            ring.at[t % slots, :, pl.ds(0, size)],
            ring_sem.at[t],
        )

    down_load = pltpu.make_async_copy(w_out, w_down, down_sem)
    for t in range(min(slots, len(tiles))):
        load(t).start()
    down_load.start()

    barrier = pltpu.get_barrier_semaphore()
    for d in range(1, seq_size):
        pl.semaphore_signal(barrier, inc=1, device_id={"seq": lax.rem(me + d, seq_size)})

    @pl.when(z > 0)
    def _():
        pl.semaphore_signal(barrier, inc=1, device_id={"mp": z - 1})

    @pl.when(z < mp_size - 1)
    def _():
        pl.semaphore_signal(barrier, inc=1, device_id={"mp": z + 1})

    pl.semaphore_wait(
        barrier, seq_size - 1 + jnp.where(z > 0, 1, 0) + jnp.where(z < mp_size - 1, 1, 0)
    )

    kv_width = keys.shape[1]
    group_count = kv_width // HEAD_SIZE
    heads = width // HEAD_SIZE // group_count
    own_rows = pl.ds(pl.multiple_of(me * rows, rows), rows)
    pieces = ((keys, 0, kv_width), (values, kv_width, kv_width), (tags, 2 * kv_width, HEAD_SIZE))

    def kv_copy(d, p):
        ref, offset, size = pieces[p]
        return pltpu.make_async_remote_copy(
            src_ref=ref, dst_ref=kv.at[own_rows, pl.ds(offset, size)],
            send_sem=kv_s.at[d - 1, p], recv_sem=kv_r.at[d - 1, p],
            device_id={"seq": lax.rem(me + d, seq_size)},
        )

    for d in range(1, seq_size):
        for p in range(3):
            kv_copy(d, p).start()
    for ref, offset, size in pieces:
        kv[own_rows, pl.ds(offset, size)] = ref[...]
    for d in range(1, seq_size):
        for p in range(3):
            kv_copy(d, p).wait()

    lane = lax.broadcasted_iota(jnp.int32, (rows, HEAD_SIZE), 1)
    own_tags = tags[...].astype(f32)
    own_docs = jnp.where(lane < HEAD_SIZE // 2, own_tags, 0.0).astype(jnp.bfloat16)
    nt = (((1,), (1,)), ((), ()))
    same = lax.dot_general(
        own_docs, kv[:, 2 * kv_width :], nt, preferred_element_type=f32
    )
    position = me * rows + lax.broadcasted_iota(jnp.int32, same.shape, 0)
    key_position = lax.broadcasted_iota(jnp.int32, same.shape, 1)
    same = jnp.where(key_position <= position, same, 0.0)
    visible = jnp.concatenate([same] * heads, axis=0) > 0.5
    square = jnp.zeros((rows, 1), f32)
    for g in range(group_count):
        first = g * heads * HEAD_SIZE
        stacked = jnp.concatenate(
            [queries[:, first + h * HEAD_SIZE : first + (h + 1) * HEAD_SIZE] for h in range(heads)],
            axis=0,
        )
        scores = lax.dot_general(
            stacked, kv[:, g * HEAD_SIZE : (g + 1) * HEAD_SIZE], nt, preferred_element_type=f32
        ) * (1.0 / math.sqrt(HEAD_SIZE))
        masked = jnp.where(visible, scores, NEG)
        top = jnp.max(masked, axis=1, keepdims=True)
        weights = jnp.where(visible, jnp.exp(masked - top), 0.0)
        total = jnp.sum(weights, axis=1, keepdims=True)
        attended = jnp.dot(
            weights.astype(jnp.bfloat16),
            kv[:, kv_width + g * HEAD_SIZE : kv_width + (g + 1) * HEAD_SIZE],
            preferred_element_type=f32,
        ) / total
        for h in range(heads):
            part_cols = pl.ds(first + h * HEAD_SIZE, HEAD_SIZE)
            low = (
                hidden[:, part_cols].astype(f32) + attended[h * rows : (h + 1) * rows]
            ).astype(jnp.bfloat16)
            resid[:, part_cols] = low
            wide = low.astype(f32)
            square = square + jnp.sum(wide * wide, axis=1, keepdims=True)
    scale = lax.rsqrt(square * (1.0 / width) + 1e-06)
    image_row = own_tags[:, HEAD_SIZE - 1 :] > 0.5
    for c in range(width // COLS):
        part_cols = pl.ds(c * COLS, COLS)
        gain = jnp.where(image_row, gains[1:2, part_cols], gains[0:1, part_cols])
        normed[:, part_cols] = (
            resid[:, part_cols].astype(f32) * scale * gain
        ).astype(jnp.bfloat16)

    target = jnp.where(me * mp_size + z >= FF // units, 1.0, 0.0)
    row_chunks = rows // CHUNK

    def place(seq_index, k):
        return x.at[pl.ds(pl.multiple_of(seq_index * rows + k * CHUNK, CHUNK), CHUNK)]

    def near_copy(k):
        return pltpu.make_async_remote_copy(
            src_ref=normed.at[pl.ds(k * CHUNK, CHUNK)], dst_ref=place(me, k),
            send_sem=near_s.at[k], recv_sem=near_r.at[k], device_id={"seq": partner},
        )

    def far_copy(d, k):
        return pltpu.make_async_remote_copy(
            src_ref=normed.at[pl.ds(k * CHUNK, CHUNK)], dst_ref=place(me, k),
            send_sem=far_s.at[d - 1, k], recv_sem=far_r.at[d - 1, k],
            device_id={"seq": peer(d)},
        )

    def relay_copy(d, k):
        return pltpu.make_async_remote_copy(
            src_ref=place(source(d), k), dst_ref=place(source(d), k),
            send_sem=relay_s.at[d - 1, k], recv_sem=relay_r.at[d - 1, k],
            device_id={"seq": partner},
        )

    keep = pltpu.make_async_copy(
        normed, x.at[pl.ds(pl.multiple_of(me * rows, rows), rows)], keep_sem
    )
    for k in range(row_chunks):
        for d in range(1, chips):
            far_copy(d, k).start()
    for k in range(row_chunks):
        near_copy(k).start()
    keep.start()

    @pl.when(z == 0)
    def _():
        right_recv[...] = jnp.zeros_like(right_recv)

    @pl.when(z == mp_size - 1)
    def _():
        left_recv[...] = jnp.zeros_like(left_recv)

    for k in range(row_chunks):
        for d in range(1, chips):
            far_copy(d, k).wait_recv()
            relay_copy(d, k).start()
    keep.wait()
    for k in range(row_chunks):
        near_copy(k).wait()
        for d in range(1, chips):
            far_copy(d, k).wait_send()
            relay_copy(d, k).wait()

    blocks = total_rows // ROW_TILE if total_rows % ROW_TILE == 0 else 1
    block_rows = total_rows // blocks
    last_dims = (((1,), (1,)), ((), ()))

    def rows_at(i):
        return pl.ds(pl.multiple_of(i * block_rows, block_rows), block_rows)

    for t, (offset, size) in enumerate(tiles):
        load(t).wait()
        slot = t % slots

        def gate_up(i, carry, slot=slot, offset=offset, size=size):
            here = x[rows_at(i), :]
            gate = lax.dot_general(
                here, ring[slot, 0, :size, :], last_dims, preferred_element_type=f32
            )
            up = lax.dot_general(
                here, ring[slot, 1, :size, :], last_dims, preferred_element_type=f32
            )
            value = gate / (1.0 + jnp.exp(-gate)) * up
            value = jnp.where(
                jnp.abs(kv[rows_at(i), kv.shape[1] - 1 :].astype(f32) - target) < 0.5, value, 0.0
            )
            act[rows_at(i), pl.ds(offset, size)] = value.astype(jnp.bfloat16)
            return carry

        lax.fori_loop(0, blocks, gate_up, 0)
        if t + slots < len(tiles):
            load(t + slots).start()
    down_load.wait()

    def cols(k):
        return pl.ds(k * COLS, COLS)

    def block_of(seq_index):
        return pl.ds(pl.multiple_of(seq_index * rows, rows), rows)

    def pair_copy(d, k):
        return pltpu.make_async_remote_copy(
            src_ref=part.at[k, block_of(lax.rem(chip + d, chips) * 2 + (1 - core))],
            dst_ref=pair_recv.at[k, d],
            send_sem=pair_s.at[d, k], recv_sem=pair_r.at[d, k],
            device_id={"seq": partner},
        )

    def cross_copy(d, k):
        return pltpu.make_async_remote_copy(
            src_ref=cross_send.at[k, d - 1], dst_ref=cross_recv.at[k, d - 1],
            send_sem=cross_s.at[d - 1, k], recv_sem=cross_r.at[d - 1, k],
            device_id={"seq": peer(d)},
        )

    def right_copy(k):
        return pltpu.make_async_remote_copy(
            src_ref=right_send.at[k], dst_ref=right_recv.at[k],
            send_sem=right_s.at[k], recv_sem=right_r.at[k], device_id={"mp": z + 1},
        )

    def left_copy(k):
        return pltpu.make_async_remote_copy(
            src_ref=left_send.at[k], dst_ref=left_recv.at[k],
            send_sem=left_s.at[k], recv_sem=left_r.at[k], device_id={"mp": z - 1},
        )

    def cross_stage(k):
        for d in range(1, chips):
            pair_copy(d, k).wait_recv()
            cross_send[k, d - 1] = (
                part[k, block_of(peer(d)), :].astype(f32) + pair_recv[k, d].astype(f32)
            ).astype(jnp.bfloat16)
            cross_copy(d, k).start()

    def gather_own(k):
        pair_copy(0, k).wait_recv()
        total = part[k, block_of(me), :].astype(f32) + pair_recv[k, 0].astype(f32)
        for d in range(1, chips):
            cross_copy(d, k).wait_recv()
            total = total + cross_recv[k, d - 1].astype(f32)
        own[k] = total

    def step_right(k):
        @pl.when(z > 0)
        def _():
            right_copy(k).wait_recv()

        @pl.when(z < mp_size - 1)
        def _():
            right_send[k] = (own[k] + right_recv[k].astype(f32)).astype(jnp.bfloat16)
            right_copy(k).start()

    def step_left(k):
        @pl.when(z < mp_size - 1)
        def _():
            left_copy(k).wait_recv()

        @pl.when(z > 0)
        def _():
            left_send[k] = (own[k] + left_recv[k].astype(f32)).astype(jnp.bfloat16)
            left_copy(k).start()

    low_half = z * 2 < mp_size
    edge = jnp.logical_or(z == 0, z == mp_size - 1)

    def finish(k):
        ffn = own[k] + right_recv[k].astype(f32) + left_recv[k].astype(f32)
        out[:, cols(k)] = (resid[:, cols(k)].astype(f32) + ffn).astype(jnp.bfloat16)

    def near_step(k):
        gather_own(k)

        @pl.when(low_half)
        def _():
            step_right(k)

        @pl.when(jnp.logical_not(low_half))
        def _():
            step_left(k)

    def far_step(k):
        @pl.when(low_half)
        def _():
            step_left(k)

        @pl.when(jnp.logical_not(low_half))
        def _():
            step_right(k)

        finish(k)

    order = list(range(1, chips)) + [0]
    for t in range(chunks + LAG + SKEW):
        if t < chunks:

            def down(i, carry, k=t):
                part[k, rows_at(i), :] = jnp.dot(
                    act[rows_at(i), :], w_down[:, cols(k)], preferred_element_type=f32
                ).astype(jnp.bfloat16)
                return carry

            lax.fori_loop(0, blocks, down, 0)
            for d in order:
                pair_copy(d, t).start()
        if 1 <= t <= chunks:
            cross_stage(t - 1)
        if SKEW <= t < chunks + SKEW:
            near_step(t - SKEW)
        if t >= LAG + SKEW:

            @pl.when(jnp.logical_not(edge))
            def _(k=t - LAG - SKEW):
                far_step(k)

    @pl.when(edge)
    def _():
        for k in range(chunks):
            far_step(k)

    for k in range(chunks):
        for d in range(chips):
            pair_copy(d, k).wait_send()
        for d in range(1, chips):
            cross_copy(d, k).wait_send()

        @pl.when(z < mp_size - 1)
        def _():
            right_copy(k).wait_send()

        @pl.when(z > 0)
        def _():
            left_copy(k).wait_send()


def layer(
    queries, keys, values, tags, hidden, gains, input_weights, output_weights, seq_size, mp_size
):
    rows, width = queries.shape
    total_rows = rows * seq_size
    units = output_weights.shape[0]
    chips = seq_size // 2
    chunks = width // COLS
    row_chunks = rows // CHUNK
    bf16 = jnp.bfloat16
    dma = pltpu.SemaphoreType.DMA
    crossing = max(chips - 1, 1)
    tiles = split_units(units)
    slots = min(SLOTS, len(tiles))
    flops = 6 * total_rows * width * units
    vmem = pl.BlockSpec(memory_space=pltpu.VMEM)
    hbm = pl.BlockSpec(memory_space=pl.ANY)
    return pl.pallas_call(
        functools.partial(ffn_kernel, seq_size, mp_size),
        out_shape=jax.ShapeDtypeStruct((rows, width), bf16),
        in_specs=[vmem] * 6 + [hbm, hbm],
        out_specs=vmem,
        scratch_shapes=[
            pltpu.VMEM((total_rows, 2 * keys.shape[1] + HEAD_SIZE), bf16),
            pltpu.VMEM((rows, width), bf16),
            pltpu.VMEM((rows, width), bf16),
            dma((seq_size - 1, 3)), dma((seq_size - 1, 3)),
            pltpu.VMEM((total_rows, width), bf16),
            pltpu.VMEM((slots, 2, tiles[0][1], width), bf16),
            pltpu.VMEM((units, width), bf16),
            pltpu.VMEM((total_rows, units), bf16),
            pltpu.VMEM((chunks, total_rows, COLS), bf16),
            pltpu.VMEM((chunks, chips, rows, COLS), bf16),
            pltpu.VMEM((chunks, crossing, rows, COLS), bf16),
            pltpu.VMEM((chunks, crossing, rows, COLS), bf16),
            pltpu.VMEM((chunks, rows, COLS), jnp.float32),
            pltpu.VMEM((chunks, rows, COLS), bf16),
            pltpu.VMEM((chunks, rows, COLS), bf16),
            pltpu.VMEM((chunks, rows, COLS), bf16),
            pltpu.VMEM((chunks, rows, COLS), bf16),
            dma((row_chunks,)), dma((row_chunks,)),
            dma((crossing, row_chunks)), dma((crossing, row_chunks)),
            dma((crossing, row_chunks)), dma((crossing, row_chunks)),
            dma(()), dma((len(tiles),)), dma(()),
            dma((chips, chunks)), dma((chips, chunks)),
            dma((crossing, chunks)), dma((crossing, chunks)),
            dma((chunks,)), dma((chunks,)), dma((chunks,)), dma((chunks,)),
        ],
        compiler_params=pltpu.CompilerParams(
            collective_id=1, has_side_effects=True, vmem_limit_bytes=58 * 1024 * 1024
        ),
        cost_estimate=pl.CostEstimate(
            flops=flops, bytes_accessed=6 * units * width, transcendentals=0
        ),
        name="layer",
    )(queries, keys, values, tags, hidden, gains, input_weights, output_weights)


def body(
    seq_size, mp_size,
    queries, keys, values, hidden_in, doc_ids, modality, input_weights, output_weights, norm_gains
):
    lane = jnp.arange(HEAD_SIZE, dtype=jnp.int32)[None, :]
    tags = jnp.where(
        lane < HEAD_SIZE // 2, lane == doc_ids[:, None], modality[:, None] == 1
    ).astype(jnp.bfloat16)
    by_unit = jnp.transpose(input_weights, (1, 2, 0))
    return layer(
        queries, keys, values, tags, hidden_in, norm_gains, by_unit, output_weights,
        seq_size, mp_size,
    )


def solution(mesh):
    rows_spec = P(("groups", "seq"), None)
    in_specs = (
        rows_spec, rows_spec, rows_spec, rows_spec,
        P(("groups", "seq")), P(("groups", "seq")),
        P(None, None, ("seq", "mp")), P(("seq", "mp"), None), P(),
    )
    f = functools.partial(body, mesh.shape["seq"], mesh.shape["mp"])
    return jax.shard_map(f, mesh=mesh, in_specs=in_specs, out_specs=rows_spec, check_vma=False)
```
